32 devices in a mesh: row: 2 (over x), col: 16 (over z, y, core).
Axes of the slice: x: 2, y: 2, z: 4, core: 2. Of those that a mesh axis runs over, the one named last changes fastest.
Arguments:
- sigma_owned: float32 [2048, 2048], P('row', 'col'), may hold values from -1 to 45, as said below
- diag_b: float32 [512, 512], replicated, may hold values from -1 to 45
- panel_b: float32 [2048, 512], P(('row', 'col')), may hold values from -0.5 to 0.5
- pattern_b: int32 [16, 4], replicated, may hold values from 0 to 1, as said below
- diag_a: float32 [512, 512], replicated, may hold values from -1 to 45
- panel_a: float32 [2048, 512], P(('row', 'col')), may hold values from -0.5 to 0.5
- pattern_a: int32 [16, 4], replicated, may hold values from 0 to 1, as said below
- coupling: float32 [512, 512], P('col'), may hold values from -0.25 to 0.25
Outputs:
- sigma_sb: float32 [2048, 512], P(('row', 'col'))
- sigma_bb: float32 [512, 512], replicated
- sigma_sa: float32 [2048, 512], P(('row', 'col'))
- sigma_ba: float32 [512, 512], replicated
- sigma_aa: float32 [512, 512], replicated
The draws below stay inside these ranges and needn't reach their ends.
Inputs may be any that keep to these rules, and one draw needn't show every extreme that they name: `sigma_owned`: the columns of a symmetric matrix, in the owner order of the first step. `pattern_b`: every block row holds at least one nonzero block. `pattern_a`: every block row holds at least one nonzero block.
All inputs are finite; a program needn't handle non-finite values.
Results may differ from the reference program's by a relative error of at most 0.000071.
Values sent between devices are 32-bit elements; how exact they have to be, the bound alone decides.
A program may use at most 64 MiB of HBM per device.

```python
import math
import jax
import jax.numpy as jnp
from jax import lax

GROUP = 64
W = 512
BLOCK = 128
NS = 2048
N_ROW = 2
N_COL = 16


def dominant(seed_key, matrix_order):
    key_off, key_diag = jax.random.split(seed_key)
    extent = 0.48 / math.sqrt(matrix_order)
    uniform_part = jax.random.uniform(key_off, (matrix_order, matrix_order), jnp.float32, -extent, extent)
    diagonal = jax.random.uniform(key_diag, (matrix_order,), jnp.float32, 0.5, 2.5)
    return (uniform_part + uniform_part.T) * 0.5 + jnp.diag(diagonal)


def block_pattern(seed_key):
    key_mask, key_pick = jax.random.split(seed_key)
    block_rows = NS // BLOCK
    block_cols = W // BLOCK
    random_mask = jax.random.randint(key_mask, (block_rows, block_cols), 0, 2, jnp.int32)
    picked = jax.random.randint(key_pick, (block_rows,), 0, block_cols, jnp.int32)
    forced = (picked[:, None] == lax.iota(jnp.int32, block_cols)[None, :]).astype(jnp.int32)
    return jnp.maximum(random_mask, forced)


def draw_sigma_owned(key, part):
    key = jax.random.fold_in(key, 1)
    matrix = dominant(key, NS)
    return matrix.reshape(NS, N_ROW, N_COL, GROUP).transpose(0, 2, 1, 3).reshape(NS, NS)


def draw_diag_b(key, part):
    key = jax.random.fold_in(key, 2)
    matrix = dominant(key, W)
    return matrix


def draw_diag_a(key, part):
    key = jax.random.fold_in(key, 3)
    matrix = dominant(key, W)
    return matrix


def draw_pattern_b(key, part):
    key = jax.random.fold_in(key, 4)
    return block_pattern(key)


def draw_pattern_a(key, part):
    key = jax.random.fold_in(key, 5)
    return block_pattern(key)


def level_of(rng, shape, cuts, least, largest):
    def one(dim, parts):
        draws = jax.random.uniform(jax.random.fold_in(jax.random.fold_in(rng, 6), dim), (parts,), jnp.float32, least / len(cuts), largest / len(cuts))
        return jnp.repeat(jnp.exp(draws), shape[dim] // parts).reshape((-1,) + (1,) * (len(shape) - dim - 1))

    level = one(*cuts[0])
    for cut in cuts[1:]:
        level = level * one(*cut)
    return level


def bell_draw(own_key, shape, width, most, cuts=(), held_as=jnp.bfloat16):
    values = width * jax.random.normal(own_key, shape, jnp.float32)
    if cuts:
        values = values * level_of(own_key, shape, cuts, -0.22, 0.18)
    return jnp.clip(values, -most, most).astype(held_as)


def setup_inputs(seed: int = 0) -> dict:
    key_of = jax.random.split(jax.random.key(seed), 9)
    sigma_owned = draw_sigma_owned(jax.random.fold_in(key_of[8], 71), 0)
    diag_b = draw_diag_b(jax.random.fold_in(key_of[8], 71), 0)
    panel_b = bell_draw(key_of[2], (NS, W), (NS // 16) ** -0.5, 0.5, ((0, 32),), jnp.float32)
    pattern_b = draw_pattern_b(jax.random.fold_in(key_of[8], 71), 0)
    diag_a = draw_diag_a(jax.random.fold_in(key_of[8], 71), 0)
    panel_a = bell_draw(key_of[5], (NS, W), (NS // 16) ** -0.5, 0.5, ((0, 32),), jnp.float32)
    pattern_a = draw_pattern_a(jax.random.fold_in(key_of[8], 71), 0)
    coupling = bell_draw(key_of[7], (W, W), W ** -0.5, 0.25, ((0, 16),), jnp.float32)
    return dict(sigma_owned=sigma_owned, diag_b=diag_b, panel_b=panel_b, pattern_b=pattern_b, diag_a=diag_a, panel_a=panel_a, pattern_a=pattern_a, coupling=coupling)


def highest(left, right):
    return jnp.dot(left, right, precision=lax.Precision.HIGHEST, preferred_element_type=jnp.float32)


def widened(pattern):
    return jnp.repeat(jnp.repeat(pattern.astype(jnp.float32), BLOCK, axis=0), BLOCK, axis=1)


def reference(sigma_owned, diag_b, panel_b, pattern_b, diag_a, panel_a, pattern_a, coupling):
    sigma_full = sigma_owned.reshape(NS, N_COL, N_ROW, GROUP).transpose(0, 2, 1, 3).reshape(NS, NS)
    masked_b = panel_b * widened(pattern_b)
    masked_a = panel_a * widened(pattern_a)
    image_b = highest(sigma_full, masked_b)
    sigma_bb = diag_b + highest(masked_b.T, image_b)
    image_as = highest(sigma_full, masked_a) - highest(image_b, coupling)
    image_ab = highest(sigma_bb, coupling) - highest(image_b.T, masked_a)
    sigma_aa = diag_a + highest(masked_a.T, image_as) + highest(coupling.T, image_ab)
    return -image_b, sigma_bb, -image_as, -image_ab, sigma_aa
```

```python
import functools

import jax
import jax.numpy as jnp
from jax import lax
from jax.experimental import pallas as pl
from jax.experimental.pallas import tpu as pltpu
from jax.sharding import PartitionSpec as P

BLOCK = 128
LANES = 128
MESH = pl.DeviceIdType.MESH


def split(x):
    high = x.astype(jnp.bfloat16)
    low = (x - high.astype(jnp.float32)).astype(jnp.bfloat16)
    return high, low


def product(left, right):
    (lh, ll), (rh, rl) = left, right
    dot = functools.partial(jnp.dot, preferred_element_type=jnp.float32)
    return dot(lh, rh) + (dot(lh, rl) + dot(ll, rh))


def masked(panel, pattern):
    rows = panel.shape[0]
    location = lax.axis_index("row") * lax.axis_size("col") + lax.axis_index("col")
    own = lax.dynamic_slice_in_dim(pattern, location * rows // BLOCK, 1, axis=0)
    return jnp.where(jnp.repeat(own, BLOCK, axis=1) == 1, panel, 0.0)


def kernel(
    R, C,
    sigma_ref, pb_ref, pa_ref, db_ref, da_ref, cp_ref,
    sb_ref, bb_ref, sa_ref, ba_ref, aa_ref,
    m, cpl, g1, g2, st, t, trecv, img, arecv, part, core_in, piece, peer_in,
    cw_send, cw_recv, ccw_send, ccw_recv, sib_send, sib_recv,
    t_send, t_recv, a_send, a_recv, c_send, c_recv, p_send, p_recv,
):
    G, W = pb_ref.shape
    NB = W // LANES
    H = C // NB
    Y = H // 2
    n = C // 2
    ncw, nccw = n // 2, (n - 1) // 2
    r = lax.axis_index("row")
    c = lax.axis_index("col")
    chip, core = c // 2, c % 2
    i_me, h = c // H, c % H
    y_me = h // 2
    sibling = c + 1 - 2 * core

    def chip_at(k):
        k = (k + n) % n
        return 2 * k + (k // (n // 2)) * (2 * (n - 1 - k) + 1 - 2 * k)

    k_me = chip // 2 + (chip % 2) * (n - 1 - 2 * (chip // 2))
    right = chip_at(k_me + 1) * 2 + core
    left = chip_at(k_me - 1) * 2 + core

    barrier = pltpu.get_barrier_semaphore()
    count = 0
    for d in range(1, C):
        pl.semaphore_signal(barrier, inc=1, device_id=(r, (c + d) % C), device_id_type=MESH)
        count += 1
    for dr in range(1, R):
        for dy in range(Y):
            peer = i_me * H + ((y_me + dy) % Y) * 2 + core
            pl.semaphore_signal(barrier, inc=1, device_id=((r + dr) % R, peer), device_id_type=MESH)
            count += 1

    slots = [
        lambda q: m.at[0, q],
        lambda q: m.at[1, q],
        lambda q: cpl.at[q],
        lambda q: g1.at[:, q],
        lambda q: g2.at[q],
    ]
    m[0, c] = pb_ref[...]
    m[1, c] = pa_ref[...]
    cpl[c] = cp_ref[...]
    pl.semaphore_wait(barrier, count)

    unsent = []

    def push(src, dst, send, recv, device):
        copy = pltpu.make_async_remote_copy(
            src_ref=src, dst_ref=dst, send_sem=send, recv_sem=recv,
            device_id=device, device_id_type=MESH,
        )
        copy.start()
        unsent.append(copy)
        return copy

    arrivals = {}

    def to_sibling(p, k, q):
        arrivals["s", p, k] = push(slots[p](q), slots[p](q), sib_send.at[p, k], sib_recv.at[p, k], (r, sibling))

    def go_right(p, s, q):
        arrivals["r", p, s] = push(slots[p](q), slots[p](q), cw_send.at[p, s], cw_recv.at[p, s], (r, right))

    def go_left(p, s, q):
        arrivals["l", p, s] = push(slots[p](q), slots[p](q), ccw_send.at[p, s], ccw_recv.at[p, s], (r, left))

    def begin(p):
        go_right(p, 0, c)
        if nccw:
            go_left(p, 0, c)
        to_sibling(p, 0, c)

    def tick(p, s):
        if s < ncw:
            q = chip_at(k_me - (s + 1)) * 2 + core
            arrivals["r", p, s].wait_recv()
            if s + 1 < ncw:
                go_right(p, s + 1, q)
            to_sibling(p, 1 + s, q)
        if s < nccw:
            q = chip_at(k_me + (s + 1)) * 2 + core
            arrivals["l", p, s].wait_recv()
            if s + 1 < nccw:
                go_left(p, s + 1, q)
            to_sibling(p, 1 + ncw + s, q)

    def settle(p):
        for k in range(n):
            arrivals["s", p, k].wait_recv()

    def multiply(p):
        rows = m.shape[1] * G
        t[p] = product((st[0], st[1]), split(m[p].reshape(rows, W)))
        for d in range(1, R):
            to = (r + d) % R
            arrivals["t", p, d] = push(
                t.at[p, pl.ds(pl.multiple_of(to * G, G), G)], trecv.at[p, d - 1],
                t_send.at[p, d - 1], t_recv.at[p, d - 1], (to, c),
            )

    def spread(p):
        total = t[p, pl.ds(pl.multiple_of(r * G, G), G)]
        for d in range(1, R):
            arrivals["t", p, d].wait_recv()
            total += trecv[p, d - 1]
        for b in range(NB):
            img[p, b] = total[:, b * LANES:(b + 1) * LANES]
        for d in range(1, NB):
            to = (i_me + d) % NB
            arrivals["a", p, d] = push(
                img.at[p, to], arecv.at[p, d - 1],
                a_send.at[p, d - 1], a_recv.at[p, d - 1], (r, to * H + h),
            )
        return total

    def image_block(p):
        blocks = [img[p, i_me]]
        for d in range(1, NB):
            arrivals["a", p, d].wait_recv()
            blocks.append(arecv[p, d - 1])
        return split(jnp.concatenate(blocks, axis=0).T)

    def gram(k, block, p):
        rows = [m[p, ((i_me + NB - d) % NB) * H + h] for d in range(NB)]
        part[k] = product(block, split(jnp.concatenate(rows, axis=0))).reshape(part.shape[1:])
        arrivals["c", k] = push(
            part.at[k, :, 1 - core], core_in.at[k], c_send.at[k], c_recv.at[k], (r, sibling)
        )

    def pair_sum(k):
        arrivals["c", k].wait_recv()
        piece[k] = part[k, :, core] + core_in[k]
        for d in range(1, R * Y):
            dr, dy = d // Y, d % Y
            y_to = (y_me + dy) % Y
            arrivals["p", k, d] = push(
                piece.at[k, y_to], peer_in.at[k, d - 1], p_send.at[k, d - 1], p_recv.at[k, d - 1],
                ((r + dr) % R, i_me * H + y_to * 2 + core),
            )

    def layer_sum(k):
        total = piece[k, y_me]
        for d in range(1, R * Y):
            arrivals["p", k, d].wait_recv()
            total += peer_in[k, d - 1]
        return total

    ticks = ncw
    half = ticks // 2
    begin(0)
    transposed = split(sigma_ref[...].T)
    st[0] = transposed[0]
    st[1] = transposed[1]
    for s in range(half):
        tick(0, s)
    begin(1)
    for s in range(half, ticks):
        tick(0, s)
        tick(1, s - half)
    settle(0)
    multiply(0)
    begin(2)
    for s in range(ticks - half, ticks):
        tick(1, s)
    image_b = spread(0)
    sb_ref[...] = -image_b
    settle(1)
    multiply(1)
    block = image_block(0)
    gram(0, block, 0)
    gram(1, block, 1)
    image_a = spread(1)
    pair_sum(0)
    pair_sum(1)
    for s in range(half):
        tick(2, s)
    gram(2, image_block(1), 1)
    g1[0, c] = layer_sum(0)
    g1[1, c] = layer_sum(1)
    begin(3)
    pair_sum(2)
    for s in range(half, ticks):
        tick(2, s)
    tick(3, 0)
    g2[c] = layer_sum(2)
    begin(4)
    settle(2)
    for s in range(1, ticks):
        tick(3, s)
        tick(4, s - 1)
    settle(3)
    tick(4, ticks - 1)
    coupling = cpl[...].reshape(W, W)
    coupled = split(coupling)
    sa_ref[...] = product(split(image_b), coupled) - image_a
    bb = db_ref[...] + g1[0].reshape(W, W)
    bb_ref[...] = bb
    cross = g1[1].reshape(W, W)
    ab = product(split(bb), coupled) - cross
    ba_ref[...] = -ab
    tail = product(split(coupling.T), split(ab)) - product(split(cross.T), coupled)
    settle(4)
    aa_ref[...] = da_ref[...] + tail + g2[...].reshape(W, W)
    for copy in unsent:
        copy.wait_send()


def shards(sigma_owned, diag_b, panel_b, pattern_b, diag_a, panel_a, pattern_a, coupling):
    R, C = lax.axis_size("row"), lax.axis_size("col")
    G, W = panel_b.shape
    NB = W // LANES
    Y = C // NB // 2
    n = C // 2
    pc = W // C
    f32, bf16 = jnp.float32, jnp.bfloat16
    shape = lambda *dims: jax.ShapeDtypeStruct(dims, f32)
    dma = pltpu.SemaphoreType.DMA
    vmem = pl.BlockSpec(memory_space=pltpu.VMEM)
    return pl.pallas_call(
        functools.partial(kernel, R, C),
        out_shape=(shape(G, W), shape(W, W), shape(G, W), shape(W, W), shape(W, W)),
        in_specs=[vmem] * 6,
        out_specs=(vmem,) * 5,
        scratch_shapes=[
            pltpu.VMEM((2, C, G, W), f32),
            pltpu.VMEM((C, coupling.shape[0], W), f32),
            pltpu.VMEM((2, C, pc, W), f32),
            pltpu.VMEM((C, pc, W), f32),
            pltpu.VMEM((2, R * G, C * G), bf16),
            pltpu.VMEM((2, R * G, W), f32),
            pltpu.VMEM((2, max(R - 1, 1), G, W), f32),
            pltpu.VMEM((2, NB, G, LANES), f32),
            pltpu.VMEM((2, NB - 1, G, LANES), f32),
            pltpu.VMEM((3, Y, 2, pc, W), f32),
            pltpu.VMEM((3, Y, pc, W), f32),
            pltpu.VMEM((3, Y, pc, W), f32),
            pltpu.VMEM((3, R * Y - 1, pc, W), f32),
            dma((5, n // 2)), dma((5, n // 2)),
            dma((5, (n - 1) // 2)), dma((5, (n - 1) // 2)),
            dma((5, n)), dma((5, n)),
            dma((2, R - 1)), dma((2, R - 1)),
            dma((2, NB - 1)), dma((2, NB - 1)),
            dma((3,)), dma((3,)),
            dma((3, R * Y - 1)), dma((3, R * Y - 1)),
        ],
        compiler_params=pltpu.CompilerParams(
            collective_id=0, has_side_effects=True, vmem_limit_bytes=48 * 1024 * 1024
        ),
    )(sigma_owned, masked(panel_b, pattern_b), masked(panel_a, pattern_a), diag_b, diag_a, coupling)


def solution(mesh):
    in_specs = (
        P("row", "col"),
        P(),
        P(("row", "col"), None),
        P(),
        P(),
        P(("row", "col"), None),
        P(),
        P("col", None),
    )
    out_specs = (P(("row", "col"), None), P(), P(("row", "col"), None), P(), P())
    return jax.shard_map(shards, mesh=mesh, in_specs=in_specs, out_specs=out_specs, check_vma=False)
```

```python
import functools

import jax
import jax.numpy as jnp
from jax import lax
from jax.experimental import pallas as pl
from jax.experimental.pallas import tpu as pltpu
from jax.sharding import PartitionSpec as P

BLOCK = 128
LANES = 128
MESH = pl.DeviceIdType.MESH


def split(x):
    high = x.astype(jnp.bfloat16)
    low = (x - high.astype(jnp.float32)).astype(jnp.bfloat16)
    return high, low


def product(left, right):
    (lh, ll), (rh, rl) = left, right
    dot = functools.partial(jnp.dot, preferred_element_type=jnp.float32)
    return dot(lh, rh) + (dot(lh, rl) + dot(ll, rh))


def kernel(
    R, C, X,
    sigma_ref, pb_ref, pa_ref, patb_ref, pata_ref, db_ref, da_ref, cp_ref,
    sb_ref, bb_ref, sa_ref, ba_ref, aa_ref,
    m, cpl, g1, g2, st, t, trecv, img, arecv, part, core_in, piece, peer_in,
    z_send, z_recv, y_send, y_recv, x_send, x_recv, sib_send, sib_recv,
    t_send, t_recv, a_send, a_recv, c_send, c_recv, p_send, p_recv,
):
    G, W = pb_ref.shape
    NB = W // LANES
    H = C // NB
    Y = H // 2
    n = C // 2
    r = lax.axis_index("row")
    c = lax.axis_index("col")
    core = c % 2
    i_me, h = c // H, c % H
    y_me = h // 2
    sibling = c + 1 - 2 * core

    barrier = pltpu.get_barrier_semaphore()
    count = 0
    for d in range(1, C):
        pl.semaphore_signal(barrier, inc=1, device_id=(r, (c + d) % C), device_id_type=MESH)
        count += 1
    for dr in range(1, R):
        for dy in range(Y):
            peer = i_me * H + ((y_me + dy) % Y) * 2 + core
            pl.semaphore_signal(barrier, inc=1, device_id=((r + dr) % R, peer), device_id_type=MESH)
            count += 1

    top, low = slice(0, G // 2), slice(G // 2, G)
    slots = [
        lambda q, x: m.at[0, q, top],
        lambda q, x: m.at[0, q, low],
        lambda q, x: m.at[1, q, top],
        lambda q, x: m.at[1, q, low],
        lambda q, x: cpl.at[q, x],
        lambda q, x: g1.at[:, q, x],
        lambda q, x: g2.at[q, x],
    ]
    B, A, CP, G1, G2 = (0, 1), (2, 3), 4, 5, 6
    x_me = r % X
    block_row = (r * C + c) * G // BLOCK
    for p, panel, pattern in ((0, pb_ref, patb_ref), (1, pa_ref, pata_ref)):
        for b in range(W // BLOCK):
            columns = slice(b * BLOCK, (b + 1) * BLOCK)
            m[p, c, :, columns] = jnp.where(pattern[block_row, b] == 1, panel[:, columns], 0.0)
    own_rows = cp_ref[...].reshape(cpl.shape[1:])
    for x in range(X):
        cpl[c, x] = own_rows[x]
    pl.semaphore_wait(barrier, count)

    unsent = []

    def push(src, dst, send, recv, device):
        copy = pltpu.make_async_remote_copy(
            src_ref=src, dst_ref=dst, send_sem=send, recv_sem=recv,
            device_id=device, device_id_type=MESH,
        )
        copy.start()
        unsent.append(copy)
        return copy

    arrivals = {}

    def slot_of(p, d, e, f=0):
        q = ((i_me + NB - d) % NB) * H + ((y_me + Y - e) % Y) * 2 + core
        return slots[p](q, (r + X - f) % X)

    def to_sibling(p, d, e, f=0):
        k = (f * Y + e) * NB + d
        ref = slot_of(p, d, e, f)
        arrivals["s", p, k] = push(ref, ref, sib_send.at[p, k], sib_recv.at[p, k], (r, sibling))

    def to_rows(p, d, e):
        if p < CP:
            return
        k = e * NB + d
        ref = slot_of(p, d, e)
        for f in range(1, X):
            arrivals["x", p, k, f] = push(
                ref, ref, x_send.at[p - CP, f - 1, k], x_recv.at[p - CP, f - 1, k], ((r + f) % R, c)
            )

    def to_group(p, d):
        ref = slot_of(p, d, 0)
        for e in range(1, Y):
            arrivals["y", p, e, d] = push(
                ref, ref, y_send.at[p, e - 1, d], y_recv.at[p, e - 1, d],
                (r, i_me * H + ((y_me + e) % Y) * 2 + core),
            )

    def begin(p):
        ref = slot_of(p, 0, 0)
        for d in range(1, NB):
            arrivals["z", p, d] = push(
                ref, ref, z_send.at[p, d - 1], z_recv.at[p, d - 1], (r, ((i_me + d) % NB) * H + h)
            )
        to_group(p, 0)
        to_rows(p, 0, 0)
        to_sibling(p, 0, 0)

    def forward_z(p):
        for d in range(1, NB):
            arrivals["z", p, d].wait_recv()
            to_group(p, d)
            to_rows(p, d, 0)
            to_sibling(p, d, 0)

    def forward_y(p):
        for d in range(NB):
            for e in range(1, Y):
                arrivals["y", p, e, d].wait_recv()
                to_rows(p, d, e)
                to_sibling(p, d, e)

    def forward_x(p):
        for f in range(1, X):
            for e in range(Y):
                for d in range(NB):
                    arrivals["x", p, e * NB + d, f].wait_recv()
                    to_sibling(p, d, e, f)

    def settle(p):
        for k in range(n * (X if p >= CP else 1)):
            arrivals["s", p, k].wait_recv()

    def multiply(p):
        rows = m.shape[1] * G
        t[p] = product((st[0], st[1]), split(m[p].reshape(rows, W)))
        for d in range(1, R):
            to = (r + d) % R
            arrivals["t", p, d] = push(
                t.at[p, pl.ds(pl.multiple_of(to * G, G), G)], trecv.at[p, d - 1],
                t_send.at[p, d - 1], t_recv.at[p, d - 1], (to, c),
            )

    def spread(p):
        total = t[p, pl.ds(pl.multiple_of(r * G, G), G)]
        for d in range(1, R):
            arrivals["t", p, d].wait_recv()
            total += trecv[p, d - 1]
        for b in range(NB):
            img[p, b] = total[:, b * LANES:(b + 1) * LANES]
        for d in range(1, NB):
            to = (i_me + d) % NB
            arrivals["a", p, d] = push(
                img.at[p, to], arecv.at[p, d - 1],
                a_send.at[p, d - 1], a_recv.at[p, d - 1], (r, to * H + h),
            )
        return total

    def image_block(p):
        blocks = [img[p, i_me]]
        for d in range(1, NB):
            arrivals["a", p, d].wait_recv()
            blocks.append(arecv[p, d - 1])
        return split(jnp.concatenate(blocks, axis=0).T)

    def gram(k, block, p):
        rows = [m[p, ((i_me + NB - d) % NB) * H + h] for d in range(NB)]
        part[k] = product(block, split(jnp.concatenate(rows, axis=0))).reshape(part.shape[1:])
        arrivals["c", k] = push(
            part.at[k, :, 1 - core], core_in.at[k], c_send.at[k], c_recv.at[k], (r, sibling)
        )

    def pair_sum(k):
        arrivals["c", k].wait_recv()
        piece[k] = (part[k, :, core] + core_in[k]).reshape(piece.shape[1:])
        for d in range(1, R * Y):
            dr, dy = d // Y, d % Y
            y_to = (y_me + dy) % Y
            r_to = (r + dr) % R
            arrivals["p", k, d] = push(
                piece.at[k, y_to, r_to % X], peer_in.at[k, d - 1], p_send.at[k, d - 1], p_recv.at[k, d - 1],
                (r_to, i_me * H + y_to * 2 + core),
            )

    def layer_sum(k):
        total = piece[k, y_me, x_me]
        for d in range(1, R * Y):
            arrivals["p", k, d].wait_recv()
            total += peer_in[k, d - 1]
        return total

    begin(0)
    begin(1)
    transposed = split(sigma_ref[...].T)
    st[0] = transposed[0]
    st[1] = transposed[1]
    forward_z(0)
    begin(2)
    forward_z(1)
    begin(3)
    forward_y(0)
    forward_y(1)
    forward_z(2)
    settle(0)
    settle(1)
    multiply(0)
    forward_z(3)
    forward_y(2)
    image_b = spread(0)
    sb_ref[...] = -image_b
    forward_y(3)
    settle(2)
    settle(3)
    multiply(1)
    begin(CP)
    block = image_block(0)
    gram(0, block, 0)
    gram(1, block, 1)
    pair_sum(0)
    pair_sum(1)
    image_a = spread(1)
    forward_z(CP)
    g1[0, c, x_me] = layer_sum(0)
    g1[1, c, x_me] = layer_sum(1)
    begin(G1)
    gram(2, image_block(1), 1)
    forward_y(CP)
    pair_sum(2)
    forward_z(G1)
    g2[c, x_me] = layer_sum(2)
    begin(G2)
    forward_x(CP)
    forward_y(G1)
    settle(CP)
    coupling = cpl[...].reshape(W, W)
    coupled = split(coupling)
    sa_ref[...] = product(split(image_b), coupled) - image_a
    forward_z(G2)
    forward_x(G1)
    forward_y(G2)
    settle(G1)
    bb = db_ref[...] + g1[0].reshape(W, W)
    bb_ref[...] = bb
    cross = g1[1].reshape(W, W)
    ab = product(split(bb), coupled) - cross
    ba_ref[...] = -ab
    forward_x(G2)
    tail = product(split(coupling.T), split(ab)) - product(split(cross.T), coupled)
    settle(G2)
    aa_ref[...] = da_ref[...] + tail + g2[...].reshape(W, W)
    for copy in unsent:
        copy.wait_send()


def shards(sigma_owned, diag_b, panel_b, pattern_b, diag_a, panel_a, pattern_a, coupling):
    R, C = lax.axis_size("row"), lax.axis_size("col")
    G, W = panel_b.shape
    NB = W // LANES
    Y = C // NB // 2
    n = C // 2
    pc = W // C
    X = R if pc % (8 * R) == 0 else 1
    px = pc // X
    f32, bf16 = jnp.float32, jnp.bfloat16
    shape = lambda *dims: jax.ShapeDtypeStruct(dims, f32)
    dma = pltpu.SemaphoreType.DMA
    vmem = pl.BlockSpec(memory_space=pltpu.VMEM)
    smem = pl.BlockSpec(memory_space=pltpu.SMEM)
    return pl.pallas_call(
        functools.partial(kernel, R, C, X),
        out_shape=(shape(G, W), shape(W, W), shape(G, W), shape(W, W), shape(W, W)),
        in_specs=[vmem] * 3 + [smem] * 2 + [vmem] * 3,
        out_specs=(vmem,) * 5,
        scratch_shapes=[
            pltpu.VMEM((2, C, G, W), f32),
            pltpu.VMEM((C, X, px, W), f32),
            pltpu.VMEM((2, C, X, px, W), f32),
            pltpu.VMEM((C, X, px, W), f32),
            pltpu.VMEM((2, R * G, C * G), bf16),
            pltpu.VMEM((2, R * G, W), f32),
            pltpu.VMEM((2, max(R - 1, 1), G, W), f32),
            pltpu.VMEM((2, NB, G, LANES), f32),
            pltpu.VMEM((2, NB - 1, G, LANES), f32),
            pltpu.VMEM((3, Y, 2, pc, W), f32),
            pltpu.VMEM((3, Y, pc, W), f32),
            pltpu.VMEM((3, Y, X, px, W), f32),
            pltpu.VMEM((3, R * Y - 1, px, W), f32),
            dma((7, NB - 1)), dma((7, NB - 1)),
            dma((7, Y - 1, NB)), dma((7, Y - 1, NB)),
            dma((3, max(X - 1, 1), n)), dma((3, max(X - 1, 1), n)),
            dma((7, n * X)), dma((7, n * X)),
            dma((2, R - 1)), dma((2, R - 1)),
            dma((2, NB - 1)), dma((2, NB - 1)),
            dma((3,)), dma((3,)),
            dma((3, R * Y - 1)), dma((3, R * Y - 1)),
        ],
        compiler_params=pltpu.CompilerParams(
            collective_id=0, has_side_effects=True, vmem_limit_bytes=48 * 1024 * 1024
        ),
    )(sigma_owned, panel_b, panel_a, pattern_b, pattern_a, diag_b, diag_a, coupling)


def solution(mesh):
    in_specs = (
        P("row", "col"),
        P(),
        P(("row", "col"), None),
        P(),
        P(),
        P(("row", "col"), None),
        P(),
        P("col", None),
    )
    out_specs = (P(("row", "col"), None), P(), P(("row", "col"), None), P(), P())
    return jax.shard_map(shards, mesh=mesh, in_specs=in_specs, out_specs=out_specs, check_vma=False)
```
